32 devices in a mesh: col: 1, row: 32 (over z, y, x, core).
Axes of the slice: x: 2, y: 2, z: 4, core: 2. Of those that a mesh axis runs over, the one named last changes fastest.
Arguments:
- tokens: bfloat16 [128, 8192], P('col', 'row'), may hold values from -6 to 6
- gate_weight: bfloat16 [8192, 14336], P('col', 'row'), may hold values from -0.0625 to 0.0625
- up_weight: bfloat16 [8192, 14336], P('col', 'row'), may hold values from -0.0625 to 0.0625
Outputs:
- hidden: bfloat16 [128, 14336], P('col', 'row')
The draws below stay inside these ranges and needn't reach their ends.
All inputs are finite; a program needn't handle non-finite values.
Results may differ from the reference program's by a relative error of at most 0.0012.
Values may be sent and summed in bfloat16 or wider, within the bound.
A program may use at most 64 MiB of HBM per device.

```python
import jax
import jax.numpy as jnp

D = 8192
FF = 14336
TOKENS = 128


def steps_of(key, shape, split, smallest, top_value):
    level = 1.0
    for axis_at, parts in split:
        heights = jax.random.uniform(jax.random.fold_in(jax.random.fold_in(key, 6), axis_at), (parts,), jnp.float32, smallest / len(split), top_value / len(split))
        level = level * jnp.repeat(jnp.exp(heights), shape[axis_at] // parts).reshape((-1,) + (1,) * (len(shape) - 1 - axis_at))
    return level


def normal_values(key, shape, spread, limit, cuts=(), kind=jnp.bfloat16):
    result = spread * jax.random.normal(key, shape, jnp.float32)
    if cuts:
        result = result * steps_of(key, shape, cuts, -0.22, 0.18)
    return jnp.clip(result, -limit, limit).astype(kind)


def setup_inputs(seed: int = 0) -> dict:
    keys = jax.random.split(jax.random.key(seed), 4)
    tokens = normal_values(keys[0], (TOKENS, D), 1.0, 6.0, ((1, 32),))
    gate_weight = normal_values(keys[1], (D, FF), D ** -0.5, 0.0625, ((1, 32),))
    up_weight = normal_values(keys[2], (D, FF), D ** -0.5, 0.0625, ((1, 32),))
    return {"tokens": tokens, "gate_weight": gate_weight, "up_weight": up_weight}


def reference(tokens, gate_weight, up_weight):
    gate = jnp.dot(tokens, gate_weight, preferred_element_type=jnp.float32)
    up = jnp.dot(tokens, up_weight, preferred_element_type=jnp.float32)
    return (jax.nn.silu(gate) * up).astype(jnp.bfloat16)
```

```python
import functools

import jax
import jax.numpy as jnp
from jax import lax
from jax.experimental import pallas as pl
from jax.experimental.pallas import tpu as pltpu
from jax.sharding import PartitionSpec as P

PLANE = 8


def dot_t(a, b):
    return lax.dot_general(a, b, (((1,), (1,)), ((), ())), preferred_element_type=jnp.float32)


def kernel(planes, tok_hbm, gate_hbm, up_hbm, out_ref, tok, gate_w, up_w, gate_acc, up_acc,
           own_sem, w_sem, send_sem, recv_sem):
    me = lax.axis_index("row")
    z = me // PLANE
    spot = me % PLANE
    core = me % 2
    x = (me // 2) % 2
    y = (me // 4) % 2
    deep = gate_hbm.shape[1] // planes
    pair = deep // (PLANE // 2)

    step_x = 2 - 4 * x
    step_y = 4 - 8 * y
    step_a = step_x + core * (step_y - step_x)
    step_b = step_y + core * (step_x - step_y)
    to_a = me + step_a
    to_b = me + step_b
    sibling = me + 1 - 2 * core

    half = z // (planes // 2)
    low = z + half * (planes - 1 - 2 * z)
    zs = [z]
    for k in range(1, planes):
        f = k - low if k == 1 else k
        zs.append(f + half * (planes - 1 - 2 * f))

    own = pltpu.make_async_copy(tok_hbm, tok.at[me], own_sem)
    own.start()

    barrier = pltpu.get_barrier_semaphore()
    partners = [zk * PLANE + spot for zk in zs[1:]] + [to_a, to_b, sibling]
    for other in partners:
        pl.semaphore_signal(barrier, inc=1, device_id={"row": other}, device_id_type=pl.DeviceIdType.MESH)

    weights = []
    for k, zk in enumerate(zs):
        rows = pl.ds(pl.multiple_of(zk * deep, deep), deep)
        pieces = [
            pltpu.make_async_copy(gate_hbm.at[:, rows], gate_w.at[:, rows], w_sem.at[k, 0]),
            pltpu.make_async_copy(up_hbm.at[:, rows], up_w.at[:, rows], w_sem.at[k, 1]),
        ]
        weights.append(pieces)

    for piece in weights[0]:
        piece.start()
    own.wait()
    pl.semaphore_wait(barrier, len(partners))

    sends = []

    def send(block, other):
        copy = pltpu.make_async_remote_copy(
            src_ref=tok.at[block],
            dst_ref=tok.at[block],
            send_sem=send_sem.at[len(sends)],
            recv_sem=recv_sem.at[block],
            device_id={"row": other},
            device_id_type=pl.DeviceIdType.MESH,
        )
        copy.start()
        sends.append(copy)

    def arrived(block):
        pltpu.make_async_remote_copy(
            src_ref=tok.at[block],
            dst_ref=tok.at[block],
            send_sem=send_sem.at[0],
            recv_sem=recv_sem.at[block],
            device_id={"row": sibling},
            device_id_type=pl.DeviceIdType.MESH,
        ).wait_recv()

    moves = {"L": 0, "A": step_a, "B": step_b, "AB": step_a + step_b}

    def block_of(kind, k):
        return zs[k] * PLANE + spot + moves[kind]

    def event(kind, k):
        block = block_of(kind, k)
        if kind != "L" or k:
            arrived(block)
        if kind == "L":
            send(block, to_a)
            send(block, to_b)
        if kind == "A":
            send(block, to_b)
        send(block, sibling)

    def compute(kind, k):
        block = block_of(kind, k)
        arrived(block + 1 - 2 * core)
        chip = block // 2
        rows = pl.ds(pl.multiple_of(chip * pair, pair), pair)
        part = jnp.concatenate([tok[2 * chip], tok[2 * chip + 1]], axis=1)
        gate = dot_t(gate_w[:, rows], part)
        up = dot_t(up_w[:, rows], part)
        if kind == "L" and k == 0:
            gate_acc[...] = gate
            up_acc[...] = up
        else:
            gate_acc[...] += gate
            up_acc[...] += up

    for zk in zs[:0:-1]:
        send(me, zk * PLANE + spot)
    event("L", 0)
    for group in weights[1:]:
        for piece in group:
            piece.start()

    order = [
        ("A", 0), ("L", 1), ("B", 0), ("AB", 0), ("A", 1), "w0", "L0", ("L", 2), "A0", ("B", 1), "B0", ("AB", 1),
        "AB0", ("A", 2), "w1", "L1", ("L", 3), "A1", ("B", 2), "B1", ("AB", 2), "AB1", ("A", 3),
        "w2", "L2", "A2", ("B", 3), "B2", "AB2", "w3", "L3", ("AB", 3), "A3", "B3", "AB3",
    ]
    for item in order:
        if isinstance(item, tuple):
            event(*item)
        elif item[0] == "w":
            for piece in weights[int(item[1])]:
                piece.wait()
        else:
            compute(item[:-1], int(item[-1]))

    gate = gate_acc[...]
    out_ref[...] = (gate / (1.0 + jnp.exp(-gate)) * up_acc[...]).astype(out_ref.dtype)
    for copy in sends:
        copy.wait_send()


def fused(parts, tokens, gate_weight, up_weight):
    planes = parts // PLANE
    rows, columns = tokens.shape[0], gate_weight.shape[0]
    return pl.pallas_call(
        functools.partial(kernel, planes),
        out_shape=jax.ShapeDtypeStruct((columns, rows), jnp.bfloat16),
        in_specs=[pl.BlockSpec(memory_space=pl.ANY)] * 3,
        out_specs=pl.BlockSpec(memory_space=pltpu.VMEM),
        scratch_shapes=[
            pltpu.VMEM((parts,) + tokens.shape, tokens.dtype),
            pltpu.VMEM(gate_weight.shape, gate_weight.dtype),
            pltpu.VMEM(up_weight.shape, up_weight.dtype),
            pltpu.VMEM((columns, rows), jnp.float32),
            pltpu.VMEM((columns, rows), jnp.float32),
            pltpu.SemaphoreType.DMA,
            pltpu.SemaphoreType.DMA((planes, 2)),
            pltpu.SemaphoreType.DMA((parts,)),
            pltpu.SemaphoreType.DMA((parts,)),
        ],
        compiler_params=pltpu.CompilerParams(
            collective_id=0, has_side_effects=True, vmem_limit_bytes=56 * 1024 * 1024
        ),
        cost_estimate=pl.CostEstimate(
            flops=4 * rows * gate_weight.size,
            bytes_accessed=4 * gate_weight.size,
            transcendentals=rows * columns,
        ),
    )(tokens, gate_weight, up_weight)


def local(mesh, tokens, gate_weight, up_weight):
    if mesh.shape["col"] > 1:
        gate_weight = lax.all_gather(gate_weight, "col", axis=0, tiled=True)
        up_weight = lax.all_gather(up_weight, "col", axis=0, tiled=True)
    parts = mesh.shape["row"]
    if parts == 4 * PLANE:
        return fused(parts, tokens, gate_weight.T, up_weight.T).T
    whole = lax.all_gather(tokens, "row", axis=1, tiled=True)
    gate = jnp.dot(whole, gate_weight, preferred_element_type=jnp.float32)
    up = jnp.dot(whole, up_weight, preferred_element_type=jnp.float32)
    return (jax.nn.silu(gate) * up).astype(jnp.bfloat16)


def solution(mesh):
    spec = P("col", "row")
    return jax.shard_map(
        functools.partial(local, mesh), mesh=mesh, in_specs=(spec, spec, spec), out_specs=spec, check_vma=False
    )
```

```python
import functools

import jax
import jax.numpy as jnp
from jax import lax
from jax.experimental import pallas as pl
from jax.experimental.pallas import tpu as pltpu
from jax.sharding import PartitionSpec as P

PLANE = 8


def dot_t(a, b):
    return lax.dot_general(a, b, (((1,), (1,)), ((), ())), preferred_element_type=jnp.float32)


def kernel(planes, tok_hbm, gate_hbm, up_hbm, out_ref, tok, weight, acc,
           own_sem, w_sem, send_sem, recv_sem):
    me = lax.axis_index("row")
    z = me // PLANE
    spot = me % PLANE
    core = me % 2
    x = (me // 2) % 2
    y = (me // 4) % 2
    deep = gate_hbm.shape[1] // planes
    units = gate_hbm.shape[0]
    pair = deep // (PLANE // 2)

    step_x = 2 - 4 * x
    step_y = 4 - 8 * y
    step_a = step_x + core * (step_y - step_x)
    step_b = step_y + core * (step_x - step_y)
    to_a = me + step_a
    to_b = me + step_b
    sibling = me + 1 - 2 * core

    half = z // (planes // 2)
    low = z + half * (planes - 1 - 2 * z)
    zs = [z]
    for k in range(1, planes):
        f = k - low if k == 1 else k
        zs.append(f + half * (planes - 1 - 2 * f))

    own = pltpu.make_async_copy(tok_hbm, tok.at[me], own_sem)
    own.start()

    barrier = pltpu.get_barrier_semaphore()
    partners = [zk * PLANE + spot for zk in zs[1:]] + [to_a, to_b, sibling]
    for other in partners:
        pl.semaphore_signal(barrier, inc=1, device_id={"row": other}, device_id_type=pl.DeviceIdType.MESH)

    weights = []
    for k, zk in enumerate(zs):
        rows = pl.ds(pl.multiple_of(zk * deep, deep), deep)
        pieces = [
            pltpu.make_async_copy(gate_hbm.at[:, rows], weight.at[pl.ds(0, units), rows], w_sem.at[k, 0]),
            pltpu.make_async_copy(up_hbm.at[:, rows], weight.at[pl.ds(units, units), rows], w_sem.at[k, 1]),
        ]
        weights.append(pieces)

    for piece in weights[0]:
        piece.start()
    own.wait()
    pl.semaphore_wait(barrier, len(partners))

    sends = []

    def send(block, other):
        copy = pltpu.make_async_remote_copy(
            src_ref=tok.at[block],
            dst_ref=tok.at[block],
            send_sem=send_sem.at[len(sends)],
            recv_sem=recv_sem.at[block],
            device_id={"row": other},
            device_id_type=pl.DeviceIdType.MESH,
        )
        copy.start()
        sends.append(copy)

    def arrived(block):
        pltpu.make_async_remote_copy(
            src_ref=tok.at[block],
            dst_ref=tok.at[block],
            send_sem=send_sem.at[0],
            recv_sem=recv_sem.at[block],
            device_id={"row": sibling},
            device_id_type=pl.DeviceIdType.MESH,
        ).wait_recv()

    moves = {"L": 0, "A": step_a, "B": step_b, "AB": step_a + step_b}

    def block_of(kind, k):
        return zs[k] * PLANE + spot + moves[kind]

    def event(kind, k):
        block = block_of(kind, k)
        if kind != "L" or k:
            arrived(block)
        if kind == "L":
            send(block, to_a)
            if k == 0:
                send(block, zs[1] * PLANE + spot)
            send(block, to_b)
            if k == 0:
                for zk in zs[2:]:
                    send(block, zk * PLANE + spot)
        if kind == "A":
            send(block, to_b)
        send(block, sibling)

    def compute(kind, k):
        block = block_of(kind, k)
        arrived(block + 1 - 2 * core)
        chip = block // 2
        rows = pl.ds(pl.multiple_of(chip * pair, pair), pair)
        part = jnp.concatenate([tok[2 * chip], tok[2 * chip + 1]], axis=1)
        both = dot_t(weight[:, rows], part)
        if kind == "L" and k == 0:
            acc[...] = both
        else:
            acc[...] += both

    event("L", 0)
    for group in weights[1:]:
        for piece in group:
            piece.start()

    order = [
        ("A", 0), ("L", 1), ("B", 0), "w0", "L0", ("A", 1), "A0", ("AB", 0), ("L", 2), "B0", ("B", 1), "AB0", ("A", 2),
        "w1", "L1", ("L", 3), "A1", ("AB", 1), "B1", ("B", 2), "AB1", ("A", 3), "w2", "L2", ("AB", 2), "A2", ("B", 3),
        "B2", "AB2", "w3", "L3", ("AB", 3), "A3", "B3", "AB3",
    ]
    for item in order:
        if isinstance(item, tuple):
            event(*item)
        elif item[0] == "w":
            for piece in weights[int(item[1])]:
                piece.wait()
        else:
            compute(item[:-1], int(item[-1]))

    gate = acc[pl.ds(0, units), :]
    out_ref[...] = (gate / (1.0 + jnp.exp(-gate)) * acc[pl.ds(units, units), :]).astype(out_ref.dtype)
    for copy in sends:
        copy.wait_send()


def fused(parts, tokens, gate_weight, up_weight):
    planes = parts // PLANE
    rows, columns = tokens.shape[0], gate_weight.shape[0]
    return pl.pallas_call(
        functools.partial(kernel, planes),
        out_shape=jax.ShapeDtypeStruct((columns, rows), jnp.bfloat16),
        in_specs=[pl.BlockSpec(memory_space=pl.ANY)] * 3,
        out_specs=pl.BlockSpec(memory_space=pltpu.VMEM),
        scratch_shapes=[
            pltpu.VMEM((parts,) + tokens.shape, tokens.dtype),
            pltpu.VMEM((2 * columns, gate_weight.shape[1]), gate_weight.dtype),
            pltpu.VMEM((2 * columns, rows), jnp.float32),
            pltpu.SemaphoreType.DMA,
            pltpu.SemaphoreType.DMA((planes, 2)),
            pltpu.SemaphoreType.DMA((parts,)),
            pltpu.SemaphoreType.DMA((parts,)),
        ],
        compiler_params=pltpu.CompilerParams(
            collective_id=0, has_side_effects=True, vmem_limit_bytes=56 * 1024 * 1024
        ),
        cost_estimate=pl.CostEstimate(
            flops=4 * rows * gate_weight.size,
            bytes_accessed=4 * gate_weight.size,
            transcendentals=rows * columns,
        ),
    )(tokens, gate_weight, up_weight)


def local(mesh, tokens, gate_weight, up_weight):
    if mesh.shape["col"] > 1:
        gate_weight = lax.all_gather(gate_weight, "col", axis=0, tiled=True)
        up_weight = lax.all_gather(up_weight, "col", axis=0, tiled=True)
    parts = mesh.shape["row"]
    if parts == 4 * PLANE:
        return fused(parts, tokens, gate_weight.T, up_weight.T).T
    whole = lax.all_gather(tokens, "row", axis=1, tiled=True)
    gate = jnp.dot(whole, gate_weight, preferred_element_type=jnp.float32)
    up = jnp.dot(whole, up_weight, preferred_element_type=jnp.float32)
    return (jax.nn.silu(gate) * up).astype(jnp.bfloat16)


def solution(mesh):
    spec = P("col", "row")
    return jax.shard_map(
        functools.partial(local, mesh), mesh=mesh, in_specs=(spec, spec, spec), out_specs=spec, check_vma=False
    )
```

```python
import functools

import jax
import jax.numpy as jnp
from jax import lax
from jax.experimental import pallas as pl
from jax.experimental.pallas import tpu as pltpu
from jax.sharding import PartitionSpec as P

PLANE = 8


def dot_t(a, b):
    return lax.dot_general(a, b, (((1,), (1,)), ((), ())), preferred_element_type=jnp.float32)


def kernel(planes, tok_hbm, gate_hbm, up_hbm, out_ref, tok, weight, acc,
           own_sem, w_sem, send_sem, recv_sem):
    me = lax.axis_index("row")
    z = me // PLANE
    spot = me % PLANE
    core = me % 2
    x = (me // 2) % 2
    y = (me // 4) % 2
    deep = gate_hbm.shape[1] // planes
    units = gate_hbm.shape[0]
    pair = deep // (PLANE // 2)

    step_x = 2 - 4 * x
    step_y = 4 - 8 * y
    step_a = step_x + core * (step_y - step_x)
    step_b = step_y + core * (step_x - step_y)
    to_a = me + step_a
    to_b = me + step_b
    sibling = me + 1 - 2 * core

    half = z // (planes // 2)
    low = z + half * (planes - 1 - 2 * z)
    zs = [z]
    for k in range(1, planes):
        f = k - low if k == 1 else k
        zs.append(f + half * (planes - 1 - 2 * f))

    own = pltpu.make_async_copy(tok_hbm, tok.at[me], own_sem)
    own.start()

    barrier = pltpu.get_barrier_semaphore()
    partners = [zk * PLANE + spot for zk in zs[1:]] + [to_a, to_b, sibling]
    for other in partners:
        pl.semaphore_signal(barrier, inc=1, device_id={"row": other}, device_id_type=pl.DeviceIdType.MESH)

    weights = []
    for k, zk in enumerate(zs):
        rows = pl.ds(pl.multiple_of(zk * deep, deep), deep)
        pieces = [
            pltpu.make_async_copy(gate_hbm.at[:, rows], weight.at[pl.ds(0, units), rows], w_sem.at[k, 0]),
            pltpu.make_async_copy(up_hbm.at[:, rows], weight.at[pl.ds(units, units), rows], w_sem.at[k, 1]),
        ]
        weights.append(pieces)

    for piece in weights[0] + weights[1]:
        piece.start()
    own.wait()
    pl.semaphore_wait(barrier, len(partners))

    sends = []

    def send(block, other):
        copy = pltpu.make_async_remote_copy(
            src_ref=tok.at[block],
            dst_ref=tok.at[block],
            send_sem=send_sem.at[len(sends)],
            recv_sem=recv_sem.at[block],
            device_id={"row": other},
            device_id_type=pl.DeviceIdType.MESH,
        )
        copy.start()
        sends.append(copy)

    def arrived(block):
        pltpu.make_async_remote_copy(
            src_ref=tok.at[block],
            dst_ref=tok.at[block],
            send_sem=send_sem.at[0],
            recv_sem=recv_sem.at[block],
            device_id={"row": sibling},
            device_id_type=pl.DeviceIdType.MESH,
        ).wait_recv()

    moves = {"L": 0, "A": step_a, "B": step_b, "AB": step_a + step_b}

    def block_of(kind, k):
        return zs[k] * PLANE + spot + moves[kind]

    def event(kind, k):
        block = block_of(kind, k)
        if kind != "L" or k:
            arrived(block)
        if kind == "L":
            send(block, to_a)
            if k == 0:
                send(block, zs[1] * PLANE + spot)
            send(block, to_b)
            if k == 0:
                for zk in zs[2:]:
                    send(block, zk * PLANE + spot)
        if kind == "A":
            send(block, to_b)
        send(block, sibling)

    def compute(kind, k):
        block = block_of(kind, k)
        arrived(block + 1 - 2 * core)
        chip = block // 2
        rows = pl.ds(pl.multiple_of(chip * pair, pair), pair)
        part = jnp.concatenate([tok[2 * chip], tok[2 * chip + 1]], axis=1)
        both = dot_t(weight[:, rows], part)
        if kind == "L" and k == 0:
            acc[...] = both
        else:
            acc[...] += both

    event("L", 0)
    later = [piece for group in weights[2:] for piece in group]

    order = [
        ("A", 0), ("L", 1), ("B", 0), "w0", "L0", ("A", 1), "A0", ("AB", 0), ("L", 2), "B0", ("B", 1), "AB0", ("A", 2),
        "w1", "L1", ("L", 3), "A1", ("AB", 1), "B1", ("B", 2), "AB1", ("A", 3), "w2", "L2", ("AB", 2), "A2", ("B", 3),
        "B2", "AB2", "w3", "L3", ("AB", 3), "A3", "B3", "AB3",
    ]
    for item in order:
        if isinstance(item, tuple):
            event(*item)
            if later:
                later.pop(0).start()
        elif item[0] == "w":
            for piece in weights[int(item[1])]:
                piece.wait()
        else:
            compute(item[:-1], int(item[-1]))

    gate = acc[pl.ds(0, units), :]
    out_ref[...] = (gate / (1.0 + jnp.exp(-gate)) * acc[pl.ds(units, units), :]).astype(out_ref.dtype)
    for copy in sends:
        copy.wait_send()


def fused(parts, tokens, gate_weight, up_weight):
    planes = parts // PLANE
    rows, columns = tokens.shape[0], gate_weight.shape[0]
    return pl.pallas_call(
        functools.partial(kernel, planes),
        out_shape=jax.ShapeDtypeStruct((columns, rows), jnp.bfloat16),
        in_specs=[pl.BlockSpec(memory_space=pl.ANY)] * 3,
        out_specs=pl.BlockSpec(memory_space=pltpu.VMEM),
        scratch_shapes=[
            pltpu.VMEM((parts,) + tokens.shape, tokens.dtype),
            pltpu.VMEM((2 * columns, gate_weight.shape[1]), gate_weight.dtype),
            pltpu.VMEM((2 * columns, rows), jnp.float32),
            pltpu.SemaphoreType.DMA,
            pltpu.SemaphoreType.DMA((planes, 2)),
            pltpu.SemaphoreType.DMA((parts,)),
            pltpu.SemaphoreType.DMA((parts,)),
        ],
        compiler_params=pltpu.CompilerParams(
            collective_id=0, has_side_effects=True, vmem_limit_bytes=56 * 1024 * 1024
        ),
        cost_estimate=pl.CostEstimate(
            flops=4 * rows * gate_weight.size,
            bytes_accessed=4 * gate_weight.size,
            transcendentals=rows * columns,
        ),
    )(tokens, gate_weight, up_weight)


def local(mesh, tokens, gate_weight, up_weight):
    if mesh.shape["col"] > 1:
        gate_weight = lax.all_gather(gate_weight, "col", axis=0, tiled=True)
        up_weight = lax.all_gather(up_weight, "col", axis=0, tiled=True)
    parts = mesh.shape["row"]
    if parts == 4 * PLANE:
        return fused(parts, tokens, gate_weight.T, up_weight.T).T
    whole = lax.all_gather(tokens, "row", axis=1, tiled=True)
    gate = jnp.dot(whole, gate_weight, preferred_element_type=jnp.float32)
    up = jnp.dot(whole, up_weight, preferred_element_type=jnp.float32)
    return (jax.nn.silu(gate) * up).astype(jnp.bfloat16)


def solution(mesh):
    spec = P("col", "row")
    return jax.shard_map(
        functools.partial(local, mesh), mesh=mesh, in_specs=(spec, spec, spec), out_specs=spec, check_vma=False
    )
```

```python
import functools
import itertools

import jax
import jax.numpy as jnp
from jax import lax
from jax.experimental import pallas as pl
from jax.experimental.pallas import tpu as pltpu
from jax.sharding import PartitionSpec as P

PLANE = 8


def dot_t(a, b):
    return lax.dot_general(a, b, (((1,), (1,)), ((), ())), preferred_element_type=jnp.float32)


def kernel(planes, tok_hbm, gate_hbm, up_hbm, out_ref, tok, weight, acc,
           own_sem, w_sem, send_sem, recv_sem):
    me = lax.axis_index("row")
    z = me // PLANE
    spot = me % PLANE
    core = me % 2
    x = (me // 2) % 2
    y = (me // 4) % 2
    deep = gate_hbm.shape[1] // planes
    units = gate_hbm.shape[0]
    pair = deep // (PLANE // 2)

    step_x = 2 - 4 * x
    step_y = 4 - 8 * y
    step_a = step_x + core * (step_y - step_x)
    step_b = step_y + core * (step_x - step_y)
    to_a = me + step_a
    to_b = me + step_b
    sibling = me + 1 - 2 * core

    half = z // (planes // 2)
    low = z + half * (planes - 1 - 2 * z)
    zs = [z]
    for k in range(1, planes):
        f = k - low if k == 1 else k
        zs.append(f + half * (planes - 1 - 2 * f))

    own = pltpu.make_async_copy(tok_hbm, tok.at[me], own_sem)
    own.start()

    barrier = pltpu.get_barrier_semaphore()
    partners = [zk * PLANE + spot for zk in zs[1:]] + [to_a, to_b, sibling]
    for other in partners:
        pl.semaphore_signal(barrier, inc=1, device_id={"row": other}, device_id_type=pl.DeviceIdType.MESH)

    weights = []
    for k, zk in enumerate(zs):
        rows = pl.ds(pl.multiple_of(zk * deep, deep), deep)
        pieces = [
            pltpu.make_async_copy(gate_hbm.at[:, rows], weight.at[pl.ds(0, units), rows], w_sem.at[k, 0]),
            pltpu.make_async_copy(up_hbm.at[:, rows], weight.at[pl.ds(units, units), rows], w_sem.at[k, 1]),
        ]
        weights.append(pieces)

    for piece in weights[0]:
        piece.start()
    own.wait()
    pl.semaphore_wait(barrier, len(partners))

    def remote(block, index, other):
        return pltpu.make_async_remote_copy(
            src_ref=tok.at[block],
            dst_ref=tok.at[block],
            send_sem=send_sem.at[index],
            recv_sem=recv_sem.at[block],
            device_id={"row": other},
            device_id_type=pl.DeviceIdType.MESH,
        )

    count = itertools.count()
    moves = {"L": 0, "A": step_a, "B": step_b, "AB": step_a + step_b}
    blocks = {(kind, k): zs[k] * PLANE + spot + move for kind, move in moves.items() for k in range(planes)}

    def send(block, other):
        remote(block, next(count), other).start()

    def event(kind, k):
        block = blocks[kind, k]
        if kind != "L" or k:
            remote(block, 0, sibling).wait_recv()
        if kind == "L":
            send(block, to_a)
            if k == 0:
                send(block, zs[1] * PLANE + spot)
            send(block, to_b)
            if k == 0:
                for zk in zs[2:]:
                    send(block, zk * PLANE + spot)
        if kind == "A":
            send(block, to_b)
        send(block, sibling)

    event("L", 0)
    for group in weights[1:]:
        for piece in group:
            piece.start()
    acc[...] = jnp.zeros_like(acc)

    steps = [
        ([("A", 0), ("L", 1), 0], ("L", 0)),
        ([("B", 0)], ("A", 0)),
        ([("A", 1), ("AB", 0), ("L", 2)], ("B", 0)),
        ([("B", 1), 1], ("L", 1)),
        ([], ("AB", 0)),
        ([("A", 2)], ("A", 1)),
        ([("L", 3), ("AB", 1)], ("B", 1)),
        ([("B", 2)], ("AB", 1)),
        ([2], ("L", 2)),
        ([], ("A", 2)),
        ([("A", 3), ("AB", 2)], ("B", 2)),
        ([("B", 3)], ("AB", 2)),
        ([3], ("L", 3)),
        ([], ("A", 3)),
        ([("AB", 3)], ("B", 3)),
        ([], ("AB", 3)),
    ]

    def take(items):
        for item in items:
            if isinstance(item, tuple):
                event(*item)
            else:
                for piece in weights[item]:
                    piece.wait()

    def body(step, carry):
        block = blocks[steps[0][1]]
        for at, (items, chip_key) in enumerate(steps):
            if items:
                pl.when(step == at)(functools.partial(take, items))
            if at:
                block = jnp.where(step == at, blocks[chip_key], block)
        remote(block + 1 - 2 * core, 0, sibling).wait_recv()
        chip = block // 2
        rows = pl.ds(pl.multiple_of(chip * pair, pair), pair)
        part = jnp.concatenate([tok[2 * chip], tok[2 * chip + 1]], axis=1)
        acc[...] += dot_t(weight[:, rows], part)
        return carry

    lax.fori_loop(0, len(steps), body, 0)

    gate = acc[pl.ds(0, units), :]
    out_ref[...] = (gate / (1.0 + jnp.exp(-gate)) * acc[pl.ds(units, units), :]).astype(out_ref.dtype)
    for index in range(next(count)):
        remote(me, index, sibling).wait_send()


def fused(parts, tokens, gate_weight, up_weight):
    planes = parts // PLANE
    rows, columns = tokens.shape[0], gate_weight.shape[0]
    return pl.pallas_call(
        functools.partial(kernel, planes),
        out_shape=jax.ShapeDtypeStruct((columns, rows), jnp.bfloat16),
        in_specs=[pl.BlockSpec(memory_space=pl.ANY)] * 3,
        out_specs=pl.BlockSpec(memory_space=pltpu.VMEM),
        scratch_shapes=[
            pltpu.VMEM((parts,) + tokens.shape, tokens.dtype),
            pltpu.VMEM((2 * columns, gate_weight.shape[1]), gate_weight.dtype),
            pltpu.VMEM((2 * columns, rows), jnp.float32),
            pltpu.SemaphoreType.DMA,
            pltpu.SemaphoreType.DMA((planes, 2)),
            pltpu.SemaphoreType.DMA((parts,)),
            pltpu.SemaphoreType.DMA((parts,)),
        ],
        compiler_params=pltpu.CompilerParams(
            collective_id=0, has_side_effects=True, vmem_limit_bytes=56 * 1024 * 1024
        ),
        cost_estimate=pl.CostEstimate(
            flops=4 * rows * gate_weight.size,
            bytes_accessed=4 * gate_weight.size,
            transcendentals=rows * columns,
        ),
    )(tokens, gate_weight, up_weight)


def local(mesh, tokens, gate_weight, up_weight):
    if mesh.shape["col"] > 1:
        gate_weight = lax.all_gather(gate_weight, "col", axis=0, tiled=True)
        up_weight = lax.all_gather(up_weight, "col", axis=0, tiled=True)
    parts = mesh.shape["row"]
    if parts == 4 * PLANE:
        return fused(parts, tokens, gate_weight.T, up_weight.T).T
    whole = lax.all_gather(tokens, "row", axis=1, tiled=True)
    gate = jnp.dot(whole, gate_weight, preferred_element_type=jnp.float32)
    up = jnp.dot(whole, up_weight, preferred_element_type=jnp.float32)
    return (jax.nn.silu(gate) * up).astype(jnp.bfloat16)


def solution(mesh):
    spec = P("col", "row")
    return jax.shard_map(
        functools.partial(local, mesh), mesh=mesh, in_specs=(spec, spec, spec), out_specs=spec, check_vma=False
    )
```

```python
import functools
import itertools

import jax
import jax.numpy as jnp
from jax import lax
from jax.experimental import pallas as pl
from jax.experimental.pallas import tpu as pltpu
from jax.sharding import PartitionSpec as P

PLANE = 8


def dot_t(a, b):
    return lax.dot_general(a, b, (((1,), (1,)), ((), ())), preferred_element_type=jnp.float32)


def kernel(planes, tok_hbm, gate_hbm, up_hbm, out_ref, tok, weight, acc,
           own_sem, w_sem, send_sem, recv_sem):
    parts = planes * PLANE
    me = lax.axis_index("row")
    z = me // PLANE
    spot = me % PLANE
    core = me % 2
    x = (me // 2) % 2
    y = (me // 4) % 2
    deep = gate_hbm.shape[1] // planes
    units = gate_hbm.shape[0]
    pair = deep // (PLANE // 2)

    step_x = 2 - 4 * x
    step_y = 4 - 8 * y
    step_a = step_x + core * (step_y - step_x)
    step_b = step_y + core * (step_x - step_y)
    to_a = me + step_a
    to_b = me + step_b
    sibling = me + 1 - 2 * core

    half = z // (planes // 2)
    low = z + half * (planes - 1 - 2 * z)
    zs = [z]
    for k in range(1, planes):
        f = k - low if k == 1 else k
        zs.append(f + half * (planes - 1 - 2 * f))

    own = pltpu.make_async_copy(tok_hbm, tok.at[me], own_sem)
    own.start()

    barrier = pltpu.get_barrier_semaphore()
    partners = [zk * PLANE + spot for zk in zs[1:]] + [to_a, to_b, sibling]
    for other in partners:
        pl.semaphore_signal(barrier, inc=1, device_id={"row": other}, device_id_type=pl.DeviceIdType.MESH)

    weights = []
    for k, zk in enumerate(zs):
        rows = pl.ds(pl.multiple_of(zk * deep, deep), deep)
        pieces = [
            pltpu.make_async_copy(gate_hbm.at[:, rows], weight.at[pl.ds(0, units), rows], w_sem.at[k, 0]),
            pltpu.make_async_copy(up_hbm.at[:, rows], weight.at[pl.ds(units, units), rows], w_sem.at[k, 1]),
        ]
        weights.append(pieces)

    for piece in weights[0]:
        piece.start()
    own.wait()
    pl.semaphore_wait(barrier, len(partners))

    def remote(block, index, other):
        return pltpu.make_async_remote_copy(
            src_ref=tok.at[block],
            dst_ref=tok.at[block],
            send_sem=send_sem.at[index],
            recv_sem=recv_sem.at[block],
            device_id={"row": other},
            device_id_type=pl.DeviceIdType.MESH,
        )

    count = itertools.count()
    moves = {"L": 0, "A": step_a, "B": step_b, "AB": step_a + step_b}
    blocks = {(kind, k): zs[k] * PLANE + spot + move for kind, move in moves.items() for k in range(planes)}

    def send(block, other):
        remote(block, next(count), other).start()

    def half(block, part, index, arrival, other):
        rows = pl.ds(part * (tok.shape[1] // 2), tok.shape[1] // 2)
        return pltpu.make_async_remote_copy(
            src_ref=tok.at[block, rows],
            dst_ref=tok.at[block, rows],
            send_sem=send_sem.at[index],
            recv_sem=recv_sem.at[arrival],
            device_id={"row": other},
            device_id_type=pl.DeviceIdType.MESH,
        )

    halves = set()

    def next_half():
        index = next(count)
        halves.add(index)
        return index

    last = planes - 1

    def event(kind, k):
        block = blocks[kind, k]
        if k == last and kind in ("A", "AB"):
            extra = parts if kind == "A" else parts + 1
            for part, arrival in enumerate((block, extra)):
                half(block, part, 0, arrival, sibling).wait_recv()
                if kind == "A":
                    half(block, part, next_half(), parts + 1 if part else block, to_b).start()
                else:
                    half(block, part, next_half(), block, sibling).start()
            if kind == "A":
                send(block, sibling)
            return
        if k == last and kind == "L":
            remote(block, 0, sibling).wait_recv()
            half(block, 0, next_half(), block, to_a).start()
            half(block, 1, next_half(), parts, to_a).start()
            send(block, to_b)
            send(block, sibling)
            return
        if kind != "L" or k:
            remote(block, 0, sibling).wait_recv()
        if kind == "L":
            send(block, to_a)
            if k == 0:
                send(block, zs[1] * PLANE + spot)
            send(block, to_b)
            if k == 0:
                for zk in zs[2:]:
                    send(block, zk * PLANE + spot)
        if kind == "A":
            send(block, to_b)
        send(block, sibling)

    event("L", 0)
    for group in weights[1:]:
        for piece in group:
            piece.start()
    acc[...] = jnp.zeros_like(acc)

    steps = [
        ([("A", 0), ("L", 1), 0], ("L", 0)),
        ([("B", 0)], ("A", 0)),
        ([("A", 1), ("AB", 0), ("L", 2)], ("B", 0)),
        ([("B", 1), 1], ("L", 1)),
        ([], ("AB", 0)),
        ([("A", 2)], ("A", 1)),
        ([("L", 3), ("AB", 1)], ("B", 1)),
        ([("B", 2)], ("AB", 1)),
        ([2], ("L", 2)),
        ([], ("A", 2)),
        ([("A", 3), ("AB", 2)], ("B", 2)),
        ([("B", 3)], ("AB", 2)),
        ([3], ("L", 3)),
        ([], ("A", 3)),
        ([("AB", 3)], ("B", 3)),
        ([], ("AB", 3)),
    ]

    def take(items):
        for item in items:
            if isinstance(item, tuple):
                event(*item)
            else:
                for piece in weights[item]:
                    piece.wait()

    def body(step, carry):
        block = blocks[steps[0][1]]
        for at, (items, chip_key) in enumerate(steps):
            if items:
                pl.when(step == at)(functools.partial(take, items))
            if at:
                block = jnp.where(step == at, blocks[chip_key], block)
        remote(block + 1 - 2 * core, 0, sibling).wait_recv()
        chip = block // 2
        rows = pl.ds(pl.multiple_of(chip * pair, pair), pair)
        part = jnp.concatenate([tok[2 * chip], tok[2 * chip + 1]], axis=1)
        acc[...] += dot_t(weight[:, rows], part)
        return carry

    lax.fori_loop(0, len(steps), body, 0)

    gate = acc[pl.ds(0, units), :]
    out_ref[...] = (gate / (1.0 + jnp.exp(-gate)) * acc[pl.ds(units, units), :]).astype(out_ref.dtype)
    for index in range(next(count)):
        if index in halves:
            half(me, 0, index, 0, sibling).wait_send()
        else:
            remote(me, index, sibling).wait_send()


def fused(parts, tokens, gate_weight, up_weight):
    planes = parts // PLANE
    rows, columns = tokens.shape[0], gate_weight.shape[0]
    return pl.pallas_call(
        functools.partial(kernel, planes),
        out_shape=jax.ShapeDtypeStruct((columns, rows), jnp.bfloat16),
        in_specs=[pl.BlockSpec(memory_space=pl.ANY)] * 3,
        out_specs=pl.BlockSpec(memory_space=pltpu.VMEM),
        scratch_shapes=[
            pltpu.VMEM((parts,) + tokens.shape, tokens.dtype),
            pltpu.VMEM((2 * columns, gate_weight.shape[1]), gate_weight.dtype),
            pltpu.VMEM((2 * columns, rows), jnp.float32),
            pltpu.SemaphoreType.DMA,
            pltpu.SemaphoreType.DMA((planes, 2)),
            pltpu.SemaphoreType.DMA((parts + 4,)),
            pltpu.SemaphoreType.DMA((parts + 2,)),
        ],
        compiler_params=pltpu.CompilerParams(
            collective_id=0, has_side_effects=True, vmem_limit_bytes=56 * 1024 * 1024
        ),
        cost_estimate=pl.CostEstimate(
            flops=4 * rows * gate_weight.size,
            bytes_accessed=4 * gate_weight.size,
            transcendentals=rows * columns,
        ),
    )(tokens, gate_weight, up_weight)


def local(mesh, tokens, gate_weight, up_weight):
    if mesh.shape["col"] > 1:
        gate_weight = lax.all_gather(gate_weight, "col", axis=0, tiled=True)
        up_weight = lax.all_gather(up_weight, "col", axis=0, tiled=True)
    parts = mesh.shape["row"]
    if parts == 4 * PLANE:
        return fused(parts, tokens, gate_weight.T, up_weight.T).T
    whole = lax.all_gather(tokens, "row", axis=1, tiled=True)
    gate = jnp.dot(whole, gate_weight, preferred_element_type=jnp.float32)
    up = jnp.dot(whole, up_weight, preferred_element_type=jnp.float32)
    return (jax.nn.silu(gate) * up).astype(jnp.bfloat16)


def solution(mesh):
    spec = P("col", "row")
    return jax.shard_map(
        functools.partial(local, mesh), mesh=mesh, in_specs=(spec, spec, spec), out_specs=spec, check_vma=False
    )
```

```python
import functools
import itertools

import jax
import jax.numpy as jnp
from jax import lax
from jax.experimental import pallas as pl
from jax.experimental.pallas import tpu as pltpu
from jax.sharding import PartitionSpec as P

PLANE = 8


def dot_t(a, b):
    return lax.dot_general(a, b, (((1,), (1,)), ((), ())), preferred_element_type=jnp.float32)


def kernel(planes, tok_hbm, gate_hbm, up_hbm, out_ref, tok, weight, acc,
           own_sem, w_sem, send_sem, recv_sem):
    parts = planes * PLANE
    me = lax.axis_index("row")
    z = me // PLANE
    spot = me % PLANE
    core = me % 2
    x = (me // 2) % 2
    y = (me // 4) % 2
    deep = gate_hbm.shape[1] // planes
    units = gate_hbm.shape[0]
    pair = deep // (PLANE // 2)

    step_x = 2 - 4 * x
    step_y = 4 - 8 * y
    step_a = step_x + core * (step_y - step_x)
    step_b = step_y + core * (step_x - step_y)
    to_a = me + step_a
    to_b = me + step_b
    sibling = me + 1 - 2 * core

    half = z // (planes // 2)
    low = z + half * (planes - 1 - 2 * z)
    zs = [z]
    for k in range(1, planes):
        f = k - low if k == 1 else k
        zs.append(f + half * (planes - 1 - 2 * f))

    own = pltpu.make_async_copy(tok_hbm, tok.at[me], own_sem)
    own.start()

    barrier = pltpu.get_barrier_semaphore()
    partners = [zk * PLANE + spot for zk in zs[1:]] + [to_a, to_b, sibling]
    for other in partners:
        pl.semaphore_signal(barrier, inc=1, device_id={"row": other}, device_id_type=pl.DeviceIdType.MESH)

    weights = []
    for k, zk in enumerate(zs):
        rows = pl.ds(pl.multiple_of(zk * deep, deep), deep)
        pieces = [
            pltpu.make_async_copy(gate_hbm.at[:, rows], weight.at[pl.ds(0, units), rows], w_sem.at[k, 0]),
            pltpu.make_async_copy(up_hbm.at[:, rows], weight.at[pl.ds(units, units), rows], w_sem.at[k, 1]),
        ]
        weights.append(pieces)

    for piece in weights[0]:
        piece.start()
    own.wait()
    pl.semaphore_wait(barrier, len(partners))

    def remote(block, index, other):
        return pltpu.make_async_remote_copy(
            src_ref=tok.at[block],
            dst_ref=tok.at[block],
            send_sem=send_sem.at[index],
            recv_sem=recv_sem.at[block],
            device_id={"row": other},
            device_id_type=pl.DeviceIdType.MESH,
        )

    count = itertools.count()
    moves = {"L": 0, "A": step_a, "B": step_b, "AB": step_a + step_b}
    blocks = {(kind, k): zs[k] * PLANE + spot + move for kind, move in moves.items() for k in range(planes)}

    def send(block, other):
        remote(block, next(count), other).start()

    def half(block, part, index, arrival, other):
        rows = pl.ds(part * (tok.shape[1] // 2), tok.shape[1] // 2)
        return pltpu.make_async_remote_copy(
            src_ref=tok.at[block, rows],
            dst_ref=tok.at[block, rows],
            send_sem=send_sem.at[index],
            recv_sem=recv_sem.at[arrival],
            device_id={"row": other},
            device_id_type=pl.DeviceIdType.MESH,
        )

    halves = set()

    def next_half():
        index = next(count)
        halves.add(index)
        return index

    last = planes - 1

    def event(kind, k):
        block = blocks[kind, k]
        if k == last and kind in ("A", "AB"):
            extra = parts if kind == "A" else parts + 1
            for part, arrival in enumerate((block, extra)):
                half(block, part, 0, arrival, sibling).wait_recv()
                if kind == "A":
                    half(block, part, next_half(), parts + 1 if part else block, to_b).start()
                else:
                    half(block, part, next_half(), block, sibling).start()
            if kind == "A":
                send(block, sibling)
            return
        if k == last and kind == "L":
            remote(block, 0, sibling).wait_recv()
            half(block, 0, next_half(), block, to_a).start()
            half(block, 1, next_half(), parts, to_a).start()
            send(block, to_b)
            send(block, sibling)
            return
        if kind != "L" or k:
            remote(block, 0, sibling).wait_recv()
        if kind == "L":
            send(block, to_a)
            if k == 0:
                send(block, zs[1] * PLANE + spot)
            send(block, to_b)
            if k == 0:
                for zk in zs[2:]:
                    send(block, zk * PLANE + spot)
        if kind == "A":
            send(block, to_b)
        send(block, sibling)

    event("L", 0)
    for group in weights[1:]:
        for piece in group:
            piece.start()
    acc[...] = jnp.zeros_like(acc)

    steps = [
        ([("A", 0), ("L", 1), 0], ("L", 0)),
        ([("B", 0)], ("A", 0)),
        ([("A", 1), ("AB", 0), ("L", 2)], ("B", 0)),
        ([("B", 1), 1], ("L", 1)),
        ([], ("AB", 0)),
        ([("A", 2)], ("A", 1)),
        ([("L", 3), ("AB", 1)], ("B", 1)),
        ([("B", 2)], ("AB", 1)),
        ([2], ("L", 2)),
        ([("A", 3), ("AB", 2)], ("A", 2)),
        ([("B", 3)], ("B", 2)),
        ([], ("AB", 2)),
        ([3], ("L", 3)),
        ([("AB", 3)], ("A", 3)),
        ([], ("B", 3)),
        ([], ("AB", 3)),
    ]

    def take(items):
        for item in items:
            if isinstance(item, tuple):
                event(*item)
            else:
                for piece in weights[item]:
                    piece.wait()

    def body(step, carry):
        block = blocks[steps[0][1]]
        for at, (items, chip_key) in enumerate(steps):
            if items:
                pl.when(step == at)(functools.partial(take, items))
            if at:
                block = jnp.where(step == at, blocks[chip_key], block)
        remote(block + 1 - 2 * core, 0, sibling).wait_recv()
        chip = block // 2
        rows = pl.ds(pl.multiple_of(chip * pair, pair), pair)
        part = jnp.concatenate([tok[2 * chip], tok[2 * chip + 1]], axis=1)
        acc[...] += dot_t(weight[:, rows], part)
        return carry

    lax.fori_loop(0, len(steps), body, 0)

    gate = acc[pl.ds(0, units), :]
    out_ref[...] = (gate / (1.0 + jnp.exp(-gate)) * acc[pl.ds(units, units), :]).astype(out_ref.dtype)
    for index in range(next(count)):
        if index in halves:
            half(me, 0, index, 0, sibling).wait_send()
        else:
            remote(me, index, sibling).wait_send()


def fused(parts, tokens, gate_weight, up_weight):
    planes = parts // PLANE
    rows, columns = tokens.shape[0], gate_weight.shape[0]
    return pl.pallas_call(
        functools.partial(kernel, planes),
        out_shape=jax.ShapeDtypeStruct((columns, rows), jnp.bfloat16),
        in_specs=[pl.BlockSpec(memory_space=pl.ANY)] * 3,
        out_specs=pl.BlockSpec(memory_space=pltpu.VMEM),
        scratch_shapes=[
            pltpu.VMEM((parts,) + tokens.shape, tokens.dtype),
            pltpu.VMEM((2 * columns, gate_weight.shape[1]), gate_weight.dtype),
            pltpu.VMEM((2 * columns, rows), jnp.float32),
            pltpu.SemaphoreType.DMA,
            pltpu.SemaphoreType.DMA((planes, 2)),
            pltpu.SemaphoreType.DMA((parts + 4,)),
            pltpu.SemaphoreType.DMA((parts + 2,)),
        ],
        compiler_params=pltpu.CompilerParams(
            collective_id=0, has_side_effects=True, vmem_limit_bytes=56 * 1024 * 1024
        ),
        cost_estimate=pl.CostEstimate(
            flops=4 * rows * gate_weight.size,
            bytes_accessed=4 * gate_weight.size,
            transcendentals=rows * columns,
        ),
    )(tokens, gate_weight, up_weight)


def local(mesh, tokens, gate_weight, up_weight):
    if mesh.shape["col"] > 1:
        gate_weight = lax.all_gather(gate_weight, "col", axis=0, tiled=True)
        up_weight = lax.all_gather(up_weight, "col", axis=0, tiled=True)
    parts = mesh.shape["row"]
    if parts == 4 * PLANE:
        return fused(parts, tokens, gate_weight.T, up_weight.T).T
    whole = lax.all_gather(tokens, "row", axis=1, tiled=True)
    gate = jnp.dot(whole, gate_weight, preferred_element_type=jnp.float32)
    up = jnp.dot(whole, up_weight, preferred_element_type=jnp.float32)
    return (jax.nn.silu(gate) * up).astype(jnp.bfloat16)


def solution(mesh):
    spec = P("col", "row")
    return jax.shard_map(
        functools.partial(local, mesh), mesh=mesh, in_specs=(spec, spec, spec), out_specs=spec, check_vma=False
    )
```
